128 devices in a mesh: dp: 8 (over z_lo, y), seq: 16 (over z_hi, x, core).
Axes of the slice: x: 4, y: 4, z: 4 (z_hi: 2, z_lo: 2; z = z_hi * 2 + z_lo), core: 2. Of those that a mesh axis runs over, the one named last changes fastest.
Arguments:
- activations: bfloat16 [8, 8192, 16384], P('dp', 'seq'), may hold values from -16 to 16
- query_weight: bfloat16 [16384, 1024], P('dp'), may hold values from -1 to 1
- kv_weight: bfloat16 [16384, 256], P('dp'), may hold values from -1 to 1
- picks: int32 [8, 128, 16], P('dp', 'seq'), may hold values from 0 to 127, as said below
Outputs:
- attended: bfloat16 [8, 8192, 1024], P('dp', 'seq')
The draws below stay inside these ranges and needn't reach their ends.
Inputs may be any that keep to these rules, and one draw needn't show every extreme that they name: `picks`: entry 0 of row b of a sequence is b; the 16 entries of row b are distinct and none exceeds max(b, 15).
All inputs are finite; a program needn't handle non-finite values.
Results may differ from the reference program's by a relative error of at most 0.0095.
Values may be sent and summed in bfloat16 or wider, within the bound.
No kernel may reach another device: no remote copies, remote signals or barrier semaphores. Data moves between devices by JAX's collectives and lax.ppermute only.
A program may use at most 192 MiB of HBM per device.

```python
import jax
import jax.numpy as jnp
from jax import lax

D = 16384
QH = 8
HD = 128
BLK = 64
PICKS = 16
SEQS = 8
LEN = 8192
NBLK = 128


def shared_columns(key):
    return jnp.clip(jax.random.normal(jax.random.fold_in(key, 11), (D, QH * HD), jnp.float32), -5.0, 5.0)


def draw_activations(key, part):
    key = jax.random.fold_in(key, 3)
    base = jnp.clip(jax.random.normal(key, (SEQS, LEN, D), jnp.float32), -6.0, 6.0)
    return base.astype(jnp.bfloat16)


def draw_query_weight(key, part):
    base = shared_columns(key)
    return (base * D ** (-0.5)).astype(jnp.bfloat16)


def draw_kv_weight(key, part):
    key = jax.random.fold_in(key, 2)
    own = jnp.clip(jax.random.normal(key, (D, 2 * HD), jnp.float32), -5.0, 5.0)
    return (own * D ** (-0.5)).astype(jnp.bfloat16)


def draw_picks(key, part):
    key = jax.random.fold_in(key, 7)
    logit_scores = jax.random.randint(key, (SEQS, NBLK, NBLK), 0, 1 << 20)
    cand = jnp.arange(NBLK).astype(jnp.int32)
    row = jnp.arange(NBLK).astype(jnp.int32)[:, None]
    limit = jnp.maximum(row, PICKS - 1)
    allowed = (cand[None, :] <= limit) & (cand[None, :] != row)
    keyed = jnp.where(allowed[None], logit_scores * NBLK + cand[None, None, :], -1)
    unused, chosen = lax.top_k(keyed, PICKS - 1)
    own = jnp.broadcast_to(row[None], (SEQS, NBLK, 1))
    return jnp.concatenate([own, chosen.astype(jnp.int32)], axis=-1).astype(jnp.int32)


def setup_inputs(seed: int = 0) -> dict:
    arg_keys = jax.random.split(jax.random.key(seed), 5)
    return {
        "activations": draw_activations(jax.random.fold_in(arg_keys[4], 71), 0),
        "query_weight": draw_query_weight(jax.random.fold_in(arg_keys[4], 71), 0),
        "kv_weight": draw_kv_weight(jax.random.fold_in(arg_keys[4], 71), 0),
        "picks": draw_picks(jax.random.fold_in(arg_keys[4], 71), 0),
    }


def rotate(vals, positions):
    half = vals.shape[-1] // 2
    freq = 500000.0 ** (-(jnp.arange(half).astype(jnp.float32) * 2.0 / vals.shape[-1]))
    angle = positions.astype(jnp.float32)[:, None] * freq[None, :]
    cosine = jnp.cos(angle)[:, None, :]
    sine = jnp.sin(angle)[:, None, :]
    first = vals[..., :half]
    second = vals[..., half:]
    return jnp.concatenate([first * cosine - second * sine, second * cosine + first * sine], axis=-1)


def reference(activations, query_weight, kv_weight, picks):
    def one_sequence(item):
        tokens, chosen = item
        query_raw = jnp.dot(tokens, query_weight, preferred_element_type=jnp.float32)
        kv_raw = jnp.dot(tokens, kv_weight, preferred_element_type=jnp.float32)
        positions = jnp.arange(LEN).astype(jnp.int32)
        query_vectors = (rotate(query_raw.reshape(LEN, QH, HD), positions) * HD ** -0.5).astype(jnp.bfloat16)
        query_vectors = query_vectors.reshape(NBLK, BLK, QH, HD)
        keys = rotate(kv_raw[:, None, :HD], positions)[:, 0].astype(jnp.bfloat16).reshape(NBLK, BLK, HD)
        values = kv_raw[:, HD:].astype(jnp.bfloat16).reshape(NBLK, BLK, HD)

        def one_block(inner):
            index, block_query, row = inner
            selected_key_rows = keys[row].reshape(PICKS * BLK, HD)
            selected_value_rows = values[row].reshape(PICKS * BLK, HD)
            logit_scores = jnp.einsum("qhd,kd->hqk", block_query.astype(jnp.float32), selected_key_rows.astype(jnp.float32))
            key_pos = (row[:, None] * BLK + jnp.arange(BLK).astype(jnp.int32)[None, :]).reshape(-1)
            query_pos = index * BLK + jnp.arange(BLK).astype(jnp.int32)
            valid = key_pos[None, None, :] <= query_pos[None, :, None]
            logit_scores = jnp.where(valid, logit_scores, -1e30)
            top = jnp.max(logit_scores, axis=-1, keepdims=True)
            weights = jnp.exp(logit_scores - top)
            probability_weights = (weights / jnp.sum(weights, axis=-1, keepdims=True)).astype(jnp.bfloat16)
            out = jnp.einsum("hqk,kd->qhd", probability_weights.astype(jnp.float32), selected_value_rows.astype(jnp.float32))
            return out.astype(jnp.bfloat16).reshape(BLK, QH * HD)

        blocks = lax.map(one_block, (jnp.arange(NBLK).astype(jnp.int32), query_vectors, chosen))
        return blocks.reshape(LEN, QH * HD)

    return lax.map(one_sequence, (activations, picks))
```

```python
import functools

import jax
import jax.numpy as jnp
from jax import lax
from jax.experimental import pallas as pl
from jax.experimental.pallas import tpu as pltpu
from jax.sharding import PartitionSpec as P

QH = 8
HD = 128
BLK = 64
PICKS = 16
SIDE = 4
AXES = ("dp", "seq")
F32 = jnp.float32
BF16 = jnp.bfloat16


def place(x, y, z, c):
    x, y, z = x % SIDE, y % SIDE, z % SIDE
    return ((z % 2) * SIDE + y) * 16 + (z // 2) * 8 + x * 2 + c


def receive_from(source):
    r = range(SIDE)
    return [
        (place(*source(x, y, z, c)), place(x, y, z, c))
        for x in r for y in r for z in r for c in range(2)
    ]


def sign(c):
    return 1 - 2 * c


FROM_Y = receive_from(lambda x, y, z, c: (x, y + sign(c), z, c))
FROM_Z = receive_from(lambda x, y, z, c: (x, y, z + sign(c), c))
FROM_X = receive_from(lambda x, y, z, c: (x + sign(c), y, z, c))
FROM_Z2 = receive_from(lambda x, y, z, c: (x, y, z + 2, c))
FROM_PAIR = receive_from(lambda x, y, z, c: (x + sign(x % 2) * sign(c), y, z, c))
FROM_CORE = receive_from(lambda x, y, z, c: (x, y, z, 1 - c))


def get(value, perm):
    return lax.ppermute(value, AXES, perm)


def rotated(raw, cosine, sine):
    return raw * cosine + pltpu.roll(raw, HD // 2, 1) * sine


def project_kernel(n, first, last, *refs):
    refs = list(refs)
    refs.pop(0)
    own, sib = refs.pop(0), refs.pop(0)
    pieces = [refs.pop(0) for _ in range(n)]
    g = pl.program_id(0)
    if not first:
        acc_own, acc_sib = refs.pop(0), refs.pop(0)
    if last:
        tables = [refs.pop(0) for _ in range(4)]
        fin_own, fin_sib = refs.pop(0), refs.pop(0)
    out_own, out_sib = refs.pop(0), refs.pop(0)
    for p in range(n):

        @pl.when(g == p)
        def _(p=p):
            for x, out, base in (
                (own, out_own, None if first else acc_own),
                (sib, out_sib, None if first else acc_sib),
            ):
                part = jnp.dot(x[...], pieces[p][...], preferred_element_type=F32)
                if p:
                    out[...] += part
                elif first:
                    out[...] = part
                else:
                    out[...] = base[...] + part

    if last:

        @pl.when(g == n - 1)
        def _():
            fin_own[...] = rotated(out_own[...], tables[0][...], tables[1][...]).astype(BF16)
            fin_sib[...] = rotated(out_sib[...], tables[2][...], tables[3][...]).astype(BF16)


def project(blocks, own, sib, pieces, acc=None, tables=None):
    n = len(pieces)
    rows = own.shape[0]
    depth, width = pieces[0].shape
    first, last = acc is None, tables is not None

    def whole(shape):
        return pl.BlockSpec(shape, lambda g, b: (0,) * len(shape))

    tile = pl.BlockSpec((rows, depth), lambda g, b: (0, b[g]))
    in_specs = [tile, tile] + [whole((depth, width))] * n
    args = [own, sib, *pieces]
    if not first:
        in_specs += [whole((rows, width))] * 2
        args += list(acc)
    scratch = []
    if last:
        in_specs += [whole((rows, width))] * 4
        args += list(tables)
        scratch = [pltpu.VMEM((rows, width), F32)] * 2
    return pl.pallas_call(
        functools.partial(project_kernel, n, first, last),
        grid_spec=pltpu.PrefetchScalarGridSpec(
            num_scalar_prefetch=1,
            grid=(n,),
            in_specs=in_specs,
            out_specs=[whole((rows, width))] * 2,
            scratch_shapes=scratch,
        ),
        out_shape=[jax.ShapeDtypeStruct((rows, width), BF16 if last else F32)] * 2,
        compiler_params=pltpu.CompilerParams(vmem_limit_bytes=40 << 20),
        cost_estimate=pl.CostEstimate(
            flops=4 * rows * depth * width * n,
            bytes_accessed=n * depth * (4 * rows + 2 * width) + 16 * rows * width,
            transcendentals=0,
        ),
    )(blocks, *args)


def attend_kernel(nblk, heads, picks, where, raw, cosine, sine, kv, out, ksel, vsel, qsel):
    def body(i, carry):
        block = where[0] + i
        core = where[3]
        for t in range(PICKS):
            pick = picks[i, t]
            chunk = pick // 16
            inside = (pick % 16) * BLK
            away_x = chunk % SIDE - where[1] + SIDE
            away_z = lax.rem(chunk // SIDE + where[2], 2)
            k_slot = lax.rem(away_x, SIDE) * 2 + away_z + core * 8
            v_slot = lax.rem(2 * SIDE - away_x, SIDE) * 2 + away_z + (1 - core) * 8
            k_row = pl.multiple_of(k_slot * 1024 + inside, BLK)
            v_row = pl.multiple_of(v_slot * 1024 + inside, BLK)
            ksel[t * BLK : (t + 1) * BLK, :] = kv[pl.ds(k_row, BLK), :]
            vsel[t * BLK : (t + 1) * BLK, :] = kv[pl.ds(v_row, BLK), :]
        rows = pl.ds(pl.multiple_of(i * BLK, BLK), BLK)
        cos, sin = cosine[rows, :], sine[rows, :]
        for h in range(heads):
            q = rotated(raw[rows, h * HD : (h + 1) * HD], cos, sin) * HD**-0.5
            qsel[h * BLK : (h + 1) * BLK, :] = q.astype(BF16)
        scores = lax.dot_general(
            ksel[...], qsel[...], (((1,), (1,)), ((), ())), preferred_element_type=F32
        )
        parts = []
        for t in range(PICKS):
            part = scores[t * BLK : (t + 1) * BLK, :]
            if t == 0:
                key = lax.broadcasted_iota(jnp.int32, part.shape, 0)
                query = lax.rem(lax.broadcasted_iota(jnp.int32, part.shape, 1), BLK)
                part = jnp.where(key <= query, part, -1e30)
            else:
                part = part + jnp.where(picks[i, t] > block, -1e30, 0.0).astype(F32)
            parts.append(part)
        scores = jnp.concatenate(parts, axis=0)
        top = jnp.max(scores, axis=0, keepdims=True)
        weights = jnp.exp(scores - top)
        total = jnp.sum(weights, axis=0, keepdims=True)
        mixed = lax.dot_general(
            vsel[...], weights.astype(BF16), (((0,), (0,)), ((), ())), preferred_element_type=F32
        )
        mixed = (mixed / total).T.astype(BF16)
        for h in range(heads):
            out[rows, h * HD : (h + 1) * HD] = mixed[h * BLK : (h + 1) * BLK, :]
        return carry

    lax.fori_loop(0, nblk, body, 0)


def attend(picks, where, raw, cosine, sine, kv):
    rows, width = raw.shape
    heads = width // HD
    nblk = rows // BLK
    smem = pl.BlockSpec(memory_space=pltpu.SMEM)
    vmem = pl.BlockSpec(memory_space=pltpu.VMEM)
    pairs = rows * heads * PICKS * BLK
    return pl.pallas_call(
        functools.partial(attend_kernel, nblk, heads),
        in_specs=[smem, smem, vmem, vmem, vmem, vmem],
        out_specs=vmem,
        out_shape=jax.ShapeDtypeStruct((rows, width), BF16),
        scratch_shapes=[
            pltpu.VMEM((PICKS * BLK, HD), BF16),
            pltpu.VMEM((PICKS * BLK, HD), BF16),
            pltpu.VMEM((heads * BLK, HD), BF16),
        ],
        compiler_params=pltpu.CompilerParams(vmem_limit_bytes=40 << 20),
        cost_estimate=pl.CostEstimate(
            flops=4 * pairs * HD, bytes_accessed=kv.size * 2 + raw.size * 8, transcendentals=pairs
        ),
    )(picks, where, raw, cosine, sine, kv)


def tables_of(first, rows):
    positions = first + jnp.arange(rows)
    half = HD // 2
    freq = 500000.0 ** (-(jnp.arange(half).astype(F32) * 2.0 / HD))
    angle = positions.astype(F32)[:, None] * freq[None, :]
    cosine, sine = jnp.cos(angle), jnp.sin(angle)
    return jnp.concatenate([cosine, cosine], 1), jnp.concatenate([-sine, sine], 1)


def local(activations, query_weight, kv_weight, picks):
    own = activations[0]
    rows = own.shape[0]
    shard = query_weight.shape[0]
    half = shard // 2
    width = query_weight.shape[1] // 2
    dp, seq = lax.axis_index("dp"), lax.axis_index("seq")
    y, z_lo = dp % SIDE, dp // SIDE
    z_hi, x, c = seq // 8, (seq // 2) % SIDE, seq % 2
    mine = x % 2
    step = 1 - 2 * c

    def block(k, flip, h):
        shard_at = (z_lo ^ flip) * SIDE + (y + step * k + 2 * SIDE) % SIDE
        return shard_at if h is None else shard_at * 2 + (mine if h == 0 else 1 - mine)

    def blocks(*names):
        return jnp.stack([block(*name) for name in names]).astype(jnp.int32)

    kv_a0 = lax.dynamic_slice(kv_weight, (0, c * HD), (shard, HD))
    sib = get(own, FROM_CORE)
    sib_picks = get(picks[0], FROM_CORE)
    kv_a1 = get(kv_a0, FROM_Y)
    kv_b0 = get(kv_a0, FROM_Z)
    kv_a2 = get(kv_a1, FROM_Y)
    kv_b1 = get(kv_a1, FROM_Z)
    kv_a3 = get(kv_a2, FROM_Y)
    kv_b2 = get(kv_a2, FROM_Z)
    kv_b3 = get(kv_a3, FROM_Z)

    a0n = lax.dynamic_slice(query_weight, (mine * half, c * width), (half, width))
    a0f = lax.dynamic_slice(query_weight, ((1 - mine) * half, c * width), (half, width))
    a1n = get(a0n, FROM_Y)
    b0n = get(a0n, FROM_Z)
    a1f = get(a1n, FROM_PAIR)
    a2n = get(a1n, FROM_Y)
    b1n = get(a1n, FROM_Z)
    a2f = get(a2n, FROM_PAIR)
    a3n = get(a2n, FROM_Y)
    b0f = get(a0f, FROM_Z)
    a3f = get(a3n, FROM_PAIR)
    b1f = get(b0f, FROM_Y)
    b2n = get(a2n, FROM_Z)
    b2f = get(b2n, FROM_PAIR)
    b3n = get(b2n, FROM_Y)
    b3f = get(a3f, FROM_Z)

    cos_own, sin_own = tables_of(seq * rows, rows)
    cos_sib, sin_sib = tables_of((seq + step) * rows, rows)
    plain = c == 1
    kv_tables = [
        jnp.where(plain, 1.0, cos_own), jnp.where(plain, 0.0, sin_own),
        jnp.where(plain, 1.0, cos_sib), jnp.where(plain, 0.0, sin_sib),
    ]
    kv_own, kv_sib = project(
        blocks(*[(k, flip, None) for flip in (0, 1) for k in range(SIDE)]),
        own, sib, [kv_a0, kv_a1, kv_a2, kv_a3, kv_b0, kv_b1, kv_b2, kv_b3],
        tables=kv_tables,
    )
    here = jnp.where(
        plain,
        jnp.concatenate([kv_sib, kv_own], 0),
        jnp.concatenate([kv_own, kv_sib], 0),
    )
    chunks = [jnp.concatenate([here, get(here, FROM_Z2)], 0)]
    for _ in range(SIDE - 1):
        chunks.append(get(chunks[-1], FROM_X))
    kv = jnp.concatenate(chunks + [get(chunk, FROM_CORE) for chunk in chunks], 0)

    acc = project(blocks((0, 0, 0), (0, 0, 1)), own, sib, [a0n, a0f])
    acc = project(blocks((1, 0, 0), (0, 1, 0)), own, sib, [a1n, b0n], acc)
    acc = project(blocks((1, 0, 1), (2, 0, 0), (1, 1, 0)), own, sib, [a1f, a2n, b1n], acc)
    acc = project(blocks((2, 0, 1), (3, 0, 0), (0, 1, 1)), own, sib, [a2f, a3n, b0f], acc)
    acc = project(blocks((3, 0, 1), (1, 1, 1), (2, 1, 0)), own, sib, [a3f, b1f, b2n], acc)
    acc = project(blocks((2, 1, 1), (3, 1, 0), (3, 1, 1)), own, sib, [b2f, b3n, b3f], acc)

    blocks_here = rows // BLK

    def where(s):
        return jnp.stack([s * blocks_here, x, z_hi, c]).astype(jnp.int32)

    out_sib = attend(sib_picks, where(seq + step), acc[1], cos_sib, sin_sib, kv)
    received = get(out_sib, FROM_CORE)
    out_own = attend(picks[0], where(seq), acc[0], cos_own, sin_own, kv)
    out = jnp.where(
        plain,
        jnp.concatenate([received, out_own], 1),
        jnp.concatenate([out_own, received], 1),
    )
    return out[None]


def solution(mesh):
    in_specs = (P("dp", "seq", None), P("dp", None), P("dp", None), P("dp", "seq", None))
    out_specs = P("dp", "seq", None)
    return jax.shard_map(local, mesh=mesh, in_specs=in_specs, out_specs=out_specs, check_vma=False)
```

```python
import functools

import jax
import jax.numpy as jnp
from jax import lax
from jax.experimental import pallas as pl
from jax.experimental.pallas import tpu as pltpu
from jax.sharding import PartitionSpec as P

QH = 8
HD = 128
BLK = 64
PICKS = 16
SIDE = 4
AXES = ("dp", "seq")
F32 = jnp.float32
BF16 = jnp.bfloat16


def place(x, y, z, c):
    x, y, z = x % SIDE, y % SIDE, z % SIDE
    return ((z % 2) * SIDE + y) * 16 + (z // 2) * 8 + x * 2 + c


def receive_from(source):
    r = range(SIDE)
    return [
        (place(*source(x, y, z, c)), place(x, y, z, c))
        for x in r for y in r for z in r for c in range(2)
    ]


def sign(c):
    return 1 - 2 * c


FROM_Y = receive_from(lambda x, y, z, c: (x, y + sign(c) * sign(x % 2), z, c))
FROM_Z = receive_from(lambda x, y, z, c: (x, y, z + sign(c), c))
FROM_X = receive_from(lambda x, y, z, c: (x + sign(c), y, z, c))
FROM_X_BACK = receive_from(lambda x, y, z, c: (x - sign(c), y, z, c))
FROM_Z2 = receive_from(lambda x, y, z, c: (x, y, z + 2, c))
FROM_PAIR = receive_from(lambda x, y, z, c: (x + sign(x % 2) * sign(c), y, z, c))
FROM_CORE = receive_from(lambda x, y, z, c: (x, y, z, 1 - c))


def get(value, perm):
    return lax.ppermute(value, AXES, perm)


fence = lax.optimization_barrier


def rotated(raw, cosine, sine):
    return raw * cosine + pltpu.roll(raw, HD // 2, 1) * sine


def project_kernel(n, first, last, *refs):
    refs = list(refs)
    refs.pop(0)
    own, sib = refs.pop(0), refs.pop(0)
    pieces = [refs.pop(0) for _ in range(n)]
    g = pl.program_id(0)
    if not first:
        acc_own, acc_sib = refs.pop(0), refs.pop(0)
    if last:
        tables = [refs.pop(0) for _ in range(4)]
        fin_own, fin_sib = refs.pop(0), refs.pop(0)
    out_own, out_sib = refs.pop(0), refs.pop(0)
    for p in range(n):

        @pl.when(g == p)
        def _(p=p):
            for x, out, base in (
                (own, out_own, None if first else acc_own),
                (sib, out_sib, None if first else acc_sib),
            ):
                part = jnp.dot(x[...], pieces[p][...], preferred_element_type=F32)
                if p:
                    out[...] += part
                elif first:
                    out[...] = part
                else:
                    out[...] = base[...] + part

    if last:

        @pl.when(g == n - 1)
        def _():
            fin_own[...] = rotated(out_own[...], tables[0][...], tables[1][...]).astype(BF16)
            fin_sib[...] = rotated(out_sib[...], tables[2][...], tables[3][...]).astype(BF16)


def project(blocks, own, sib, pieces, acc=None, tables=None):
    n = len(pieces)
    rows = own.shape[0]
    depth, width = pieces[0].shape
    first, last = acc is None, tables is not None

    def whole(shape):
        return pl.BlockSpec(shape, lambda g, b: (0,) * len(shape))

    tile = pl.BlockSpec((rows, depth), lambda g, b: (0, b[g]))
    in_specs = [tile, tile] + [whole((depth, width))] * n
    args = [own, sib, *pieces]
    if not first:
        in_specs += [whole((rows, width))] * 2
        args += list(acc)
    scratch = []
    if last:
        in_specs += [whole((rows, width))] * 4
        args += list(tables)
        scratch = [pltpu.VMEM((rows, width), F32)] * 2
    return pl.pallas_call(
        functools.partial(project_kernel, n, first, last),
        grid_spec=pltpu.PrefetchScalarGridSpec(
            num_scalar_prefetch=1,
            grid=(n,),
            in_specs=in_specs,
            out_specs=[whole((rows, width))] * 2,
            scratch_shapes=scratch,
        ),
        out_shape=[jax.ShapeDtypeStruct((rows, width), BF16 if last else F32)] * 2,
        compiler_params=pltpu.CompilerParams(vmem_limit_bytes=56 << 20),
        cost_estimate=pl.CostEstimate(
            flops=4 * rows * depth * width * n,
            bytes_accessed=n * depth * (4 * rows + 2 * width) + 16 * rows * width,
            transcendentals=0,
        ),
    )(blocks, *args)


def query_kernel(n, first, blocks, own, sib, *refs):
    pieces, refs = refs[:n], refs[n:]
    bases, (out_own, out_sib, held, sems) = refs[:-4], refs[-4:]
    g = pl.program_id(0)

    def fetch(p):
        return pltpu.make_async_copy(pieces[p], held.at[p % 2], sems.at[p % 2])

    for p in range(n):

        @pl.when(g == p)
        def _(p=p):
            if p == 0:
                fetch(0).start()
            if p + 1 < n:
                fetch(p + 1).start()
            fetch(p).wait()
            for i, (x, out) in enumerate(((own, out_own), (sib, out_sib))):
                part = jnp.dot(x[...], held[p % 2], preferred_element_type=F32)
                if p:
                    out[...] += part
                elif first:
                    out[...] = part
                else:
                    out[...] = bases[i][...] + part


def project_query(blocks, own, sib, pieces, acc=()):
    n = len(pieces)
    rows = own.shape[0]
    depth, width = pieces[0].shape
    tile = pl.BlockSpec((rows, depth), lambda g, b: (0, b[g]))
    result = pl.BlockSpec((rows, width), lambda g, b: (0, 0))
    return pl.pallas_call(
        functools.partial(query_kernel, n, not acc),
        grid_spec=pltpu.PrefetchScalarGridSpec(
            num_scalar_prefetch=1,
            grid=(n,),
            in_specs=[tile, tile]
            + [pl.BlockSpec(memory_space=pl.ANY)] * n
            + [result] * len(acc),
            out_specs=[result] * 2,
            scratch_shapes=[pltpu.VMEM((2, depth, width), BF16), pltpu.SemaphoreType.DMA((2,))],
        ),
        out_shape=[jax.ShapeDtypeStruct((rows, width), F32)] * 2,
        compiler_params=pltpu.CompilerParams(vmem_limit_bytes=40 << 20),
        cost_estimate=pl.CostEstimate(
            flops=4 * rows * depth * width * n,
            bytes_accessed=n * depth * (4 * rows + 2 * width) + 16 * rows * width,
            transcendentals=0,
        ),
    )(blocks, own, sib, *pieces, *acc)


def attend_kernel(nblk, heads, picks, where, raw, cosine, sine, kv, out, ksel, vsel, qsel):
    def body(i, carry):
        block = where[0] + i
        core = where[3]
        for t in range(PICKS):
            pick = picks[i, t]
            chunk = pick // 16
            inside = (pick % 16) * BLK
            away_x = chunk % SIDE - where[1] + SIDE
            away_z = lax.rem(chunk // SIDE + where[2], 2)
            k_slot = lax.rem(away_x, SIDE) * 2 + away_z + core * 8
            v_slot = lax.rem(2 * SIDE - away_x, SIDE) * 2 + away_z + (1 - core) * 8
            k_row = pl.multiple_of(k_slot * 1024 + inside, BLK)
            v_row = pl.multiple_of(v_slot * 1024 + inside, BLK)
            ksel[t * BLK : (t + 1) * BLK, :] = kv[pl.ds(k_row, BLK), :]
            vsel[t * BLK : (t + 1) * BLK, :] = kv[pl.ds(v_row, BLK), :]
        rows = pl.ds(pl.multiple_of(i * BLK, BLK), BLK)
        cos, sin = cosine[rows, :], sine[rows, :]
        for h in range(heads):
            q = rotated(raw[rows, h * HD : (h + 1) * HD], cos, sin) * HD**-0.5
            qsel[h * BLK : (h + 1) * BLK, :] = q.astype(BF16)
        scores = lax.dot_general(
            ksel[...], qsel[...], (((1,), (1,)), ((), ())), preferred_element_type=F32
        )
        parts = []
        for t in range(PICKS):
            part = scores[t * BLK : (t + 1) * BLK, :]
            if t == 0:
                key = lax.broadcasted_iota(jnp.int32, part.shape, 0)
                query = lax.rem(lax.broadcasted_iota(jnp.int32, part.shape, 1), BLK)
                part = jnp.where(key <= query, part, -1e30)
            else:
                part = part + jnp.where(picks[i, t] > block, -1e30, 0.0).astype(F32)
            parts.append(part)
        scores = jnp.concatenate(parts, axis=0)
        top = jnp.max(scores, axis=0, keepdims=True)
        weights = jnp.exp(scores - top)
        total = jnp.sum(weights, axis=0, keepdims=True)
        mixed = lax.dot_general(
            vsel[...], weights.astype(BF16), (((0,), (0,)), ((), ())), preferred_element_type=F32
        )
        mixed = (mixed / total).T.astype(BF16)
        for h in range(heads):
            out[rows, h * HD : (h + 1) * HD] = mixed[h * BLK : (h + 1) * BLK, :]
        return carry

    lax.fori_loop(0, nblk, body, 0)


def attend(picks, where, raw, cosine, sine, kv):
    rows, width = raw.shape
    heads = width // HD
    nblk = rows // BLK
    smem = pl.BlockSpec(memory_space=pltpu.SMEM)
    vmem = pl.BlockSpec(memory_space=pltpu.VMEM)
    pairs = rows * heads * PICKS * BLK
    return pl.pallas_call(
        functools.partial(attend_kernel, nblk, heads),
        in_specs=[smem, smem, vmem, vmem, vmem, vmem],
        out_specs=vmem,
        out_shape=jax.ShapeDtypeStruct((rows, width), BF16),
        scratch_shapes=[
            pltpu.VMEM((PICKS * BLK, HD), BF16),
            pltpu.VMEM((PICKS * BLK, HD), BF16),
            pltpu.VMEM((heads * BLK, HD), BF16),
        ],
        compiler_params=pltpu.CompilerParams(vmem_limit_bytes=40 << 20),
        cost_estimate=pl.CostEstimate(
            flops=4 * pairs * HD, bytes_accessed=kv.size * 2 + raw.size * 8, transcendentals=pairs
        ),
    )(picks, where, raw, cosine, sine, kv)


def tables_of(first, rows):
    positions = first + jnp.arange(rows)
    half = HD // 2
    freq = 500000.0 ** (-(jnp.arange(half).astype(F32) * 2.0 / HD))
    angle = positions.astype(F32)[:, None] * freq[None, :]
    cosine, sine = jnp.cos(angle), jnp.sin(angle)
    return jnp.concatenate([cosine, cosine], 1), jnp.concatenate([-sine, sine], 1)


def local(activations, query_weight, kv_weight, picks):
    own = activations[0]
    rows = own.shape[0]
    shard = query_weight.shape[0]
    width = query_weight.shape[1] // 2
    dp, seq = lax.axis_index("dp"), lax.axis_index("seq")
    y, z_lo = dp % SIDE, dp // SIDE
    z_hi, x, c = seq // 8, (seq // 2) % SIDE, seq % 2
    step = 1 - 2 * c
    along = step * (1 - 2 * (x % 2))

    def blocks(*names):
        return jnp.stack(
            [(z_lo ^ flip) * SIDE + (y + along * k + SIDE) % SIDE for k, flip in names]
        ).astype(jnp.int32)

    kv_a0 = lax.dynamic_slice(kv_weight, (0, c * HD), (shard, HD))
    sib = get(own, FROM_CORE)
    sib_picks = get(picks[0], FROM_CORE)
    kv_a1 = get(kv_a0, FROM_Y)
    kv_b0 = get(kv_a0, FROM_Z)
    kv_a2 = get(kv_a1, FROM_Y)
    kv_b1 = get(kv_a1, FROM_Z)
    kv_a3 = get(kv_a2, FROM_Y)
    kv_b2 = get(kv_a2, FROM_Z)
    kv_b3 = get(kv_a3, FROM_Z)

    a0 = lax.dynamic_slice(query_weight, (0, c * width), (shard, width))
    a1 = get(a0, FROM_Y)
    b0 = get(a0, FROM_Z)
    a2 = get(a1, FROM_Y)
    b1 = get(a1, FROM_Z)
    a3 = get(a1, FROM_PAIR)
    b2 = get(b1, FROM_Y)
    b3 = get(a3, FROM_Z)

    cos_own, sin_own = tables_of(seq * rows, rows)
    cos_sib, sin_sib = tables_of((seq + step) * rows, rows)
    plain = c == 1
    kv_tables = [
        jnp.where(plain, 1.0, cos_own), jnp.where(plain, 0.0, sin_own),
        jnp.where(plain, 1.0, cos_sib), jnp.where(plain, 0.0, sin_sib),
    ]
    kv_own, kv_sib = project(
        blocks(*[(k, flip) for flip in (0, 1) for k in range(SIDE)]),
        own, sib, [kv_a0, kv_a1, kv_a2, kv_a3, kv_b0, kv_b1, kv_b2, kv_b3],
        tables=kv_tables,
    )
    here = jnp.where(
        plain,
        jnp.concatenate([kv_sib, kv_own], 0),
        jnp.concatenate([kv_own, kv_sib], 0),
    )
    near = jnp.concatenate([here, get(here, FROM_Z2)], 0)
    ahead, back = fence((get(near, FROM_X), get(near, FROM_X_BACK)))
    chunks = [near, ahead, get(ahead, FROM_X), back]
    kv = jnp.concatenate(chunks + [get(chunk, FROM_CORE) for chunk in chunks], 0)

    acc = project_query(blocks((0, 0), (1, 0), (0, 1)), own, sib, [a0, a1, b0])
    acc = project_query(blocks((2, 0), (3, 0), (1, 1)), own, sib, [a2, a3, b1], acc)
    acc = project_query(blocks((2, 1), (3, 1)), own, sib, [b2, b3], acc)

    blocks_here = rows // BLK

    def where(s):
        return jnp.stack([s * blocks_here, x, z_hi, c]).astype(jnp.int32)

    out_sib = attend(sib_picks, where(seq + step), acc[1], cos_sib, sin_sib, kv)
    received = get(out_sib, FROM_CORE)
    out_own = attend(picks[0], where(seq), acc[0], cos_own, sin_own, kv)
    out = jnp.where(
        plain,
        jnp.concatenate([received, out_own], 1),
        jnp.concatenate([out_own, received], 1),
    )
    return out[None]


def solution(mesh):
    in_specs = (P("dp", "seq", None), P("dp", None), P("dp", None), P("dp", "seq", None))
    out_specs = P("dp", "seq", None)
    return jax.shard_map(local, mesh=mesh, in_specs=in_specs, out_specs=out_specs, check_vma=False)
```

```python
import functools

import jax
import jax.numpy as jnp
from jax import lax
from jax.experimental import pallas as pl
from jax.experimental.pallas import tpu as pltpu
from jax.sharding import PartitionSpec as P

QH = 8
HD = 128
BLK = 64
PICKS = 16
SIDE = 4
AXES = ("dp", "seq")
F32 = jnp.float32
BF16 = jnp.bfloat16


def place(x, y, z, c):
    x, y, z = x % SIDE, y % SIDE, z % SIDE
    return ((z % 2) * SIDE + y) * 16 + (z // 2) * 8 + x * 2 + c


def receive_from(source):
    r = range(SIDE)
    return [
        (place(*source(x, y, z, c)), place(x, y, z, c))
        for x in r for y in r for z in r for c in range(2)
    ]


def sign(c):
    return 1 - 2 * c


FROM_Y = receive_from(lambda x, y, z, c: (x, y + sign(c) * sign(x % 2), z, c))
FROM_Z = receive_from(lambda x, y, z, c: (x, y, z + sign(c), c))
FROM_X = receive_from(lambda x, y, z, c: (x + sign(c), y, z, c))
FROM_X_BACK = receive_from(lambda x, y, z, c: (x - sign(c), y, z, c))
FROM_Z2 = receive_from(lambda x, y, z, c: (x, y, z + 2, c))
FROM_PAIR = receive_from(lambda x, y, z, c: (x + sign(x % 2) * sign(c), y, z, c))
FROM_CORE = receive_from(lambda x, y, z, c: (x, y, z, 1 - c))


def get(value, perm):
    return lax.ppermute(value, AXES, perm)


fence = lax.optimization_barrier


def rotated(raw, cosine, sine):
    return raw * cosine + pltpu.roll(raw, HD // 2, 1) * sine


def project_kernel(n, first, last, *refs):
    refs = list(refs)
    refs.pop(0)
    own, sib = refs.pop(0), refs.pop(0)
    pieces = [refs.pop(0) for _ in range(n)]
    g = pl.program_id(0)
    if not first:
        acc_own, acc_sib = refs.pop(0), refs.pop(0)
    if last:
        tables = [refs.pop(0) for _ in range(4)]
        fin_own, fin_sib = refs.pop(0), refs.pop(0)
    out_own, out_sib = refs.pop(0), refs.pop(0)
    for p in range(n):

        @pl.when(g == p)
        def _(p=p):
            for x, out, base in (
                (own, out_own, None if first else acc_own),
                (sib, out_sib, None if first else acc_sib),
            ):
                part = jnp.dot(x[...], pieces[p][...], preferred_element_type=F32)
                if p:
                    out[...] += part
                elif first:
                    out[...] = part
                else:
                    out[...] = base[...] + part

    if last:

        @pl.when(g == n - 1)
        def _():
            fin_own[...] = rotated(out_own[...], tables[0][...], tables[1][...]).astype(BF16)
            fin_sib[...] = rotated(out_sib[...], tables[2][...], tables[3][...]).astype(BF16)


def project(blocks, own, sib, pieces, acc=None, tables=None):
    n = len(pieces)
    rows = own.shape[0]
    depth, width = pieces[0].shape
    first, last = acc is None, tables is not None

    def whole(shape):
        return pl.BlockSpec(shape, lambda g, b: (0,) * len(shape))

    tile = pl.BlockSpec((rows, depth), lambda g, b: (0, b[g]))
    in_specs = [tile, tile] + [whole((depth, width))] * n
    args = [own, sib, *pieces]
    if not first:
        in_specs += [whole((rows, width))] * 2
        args += list(acc)
    scratch = []
    if last:
        in_specs += [whole((rows, width))] * 4
        args += list(tables)
        scratch = [pltpu.VMEM((rows, width), F32)] * 2
    return pl.pallas_call(
        functools.partial(project_kernel, n, first, last),
        grid_spec=pltpu.PrefetchScalarGridSpec(
            num_scalar_prefetch=1,
            grid=(n,),
            in_specs=in_specs,
            out_specs=[whole((rows, width))] * 2,
            scratch_shapes=scratch,
        ),
        out_shape=[jax.ShapeDtypeStruct((rows, width), BF16 if last else F32)] * 2,
        compiler_params=pltpu.CompilerParams(vmem_limit_bytes=56 << 20),
        cost_estimate=pl.CostEstimate(
            flops=4 * rows * depth * width * n,
            bytes_accessed=n * depth * (4 * rows + 2 * width) + 16 * rows * width,
            transcendentals=0,
        ),
    )(blocks, *args)


def query_kernel(n, first, blocks, own, sib, *refs):
    pieces, refs = refs[:n], refs[n:]
    bases, (out_own, out_sib, held, sems) = refs[:-4], refs[-4:]
    g = pl.program_id(0)

    def fetch(p):
        return pltpu.make_async_copy(pieces[p], held.at[p % 2], sems.at[p % 2])

    for p in range(n):

        @pl.when(g == p)
        def _(p=p):
            if p == 0:
                fetch(0).start()
            if p + 1 < n:
                fetch(p + 1).start()
            fetch(p).wait()
            for i, (x, out) in enumerate(((own, out_own), (sib, out_sib))):
                part = jnp.dot(x[...], held[p % 2], preferred_element_type=F32)
                if p:
                    out[...] += part
                elif first:
                    out[...] = part
                else:
                    out[...] = bases[i][...] + part


def project_query(blocks, own, sib, pieces, acc=()):
    n = len(pieces)
    rows = own.shape[0]
    depth, width = pieces[0].shape
    tile = pl.BlockSpec((rows, depth), lambda g, b: (0, b[g]))
    result = pl.BlockSpec((rows, width), lambda g, b: (0, 0))
    return pl.pallas_call(
        functools.partial(query_kernel, n, not acc),
        grid_spec=pltpu.PrefetchScalarGridSpec(
            num_scalar_prefetch=1,
            grid=(n,),
            in_specs=[tile, tile]
            + [pl.BlockSpec(memory_space=pl.ANY)] * n
            + [result] * len(acc),
            out_specs=[result] * 2,
            scratch_shapes=[pltpu.VMEM((2, depth, width), BF16), pltpu.SemaphoreType.DMA((2,))],
        ),
        out_shape=[jax.ShapeDtypeStruct((rows, width), F32)] * 2,
        compiler_params=pltpu.CompilerParams(vmem_limit_bytes=40 << 20),
        cost_estimate=pl.CostEstimate(
            flops=4 * rows * depth * width * n,
            bytes_accessed=n * depth * (4 * rows + 2 * width) + 16 * rows * width,
            transcendentals=0,
        ),
    )(blocks, own, sib, *pieces, *acc)


def attend_kernel(nblk, heads, picks, where, raw, cosine, sine, kv, out, ksel, vsel, qsel):
    def body(i, carry):
        block = where[0] + i
        core = where[3]
        for t in range(PICKS):
            pick = picks[i, t]
            chunk = pick // 16
            inside = (pick % 16) * BLK
            away_x = chunk % SIDE - where[1] + SIDE
            away_z = lax.rem(chunk // SIDE + where[2], 2)
            k_slot = lax.rem(away_x, SIDE) * 2 + away_z + core * 8
            v_slot = lax.rem(2 * SIDE - away_x, SIDE) * 2 + away_z + (1 - core) * 8
            k_row = pl.multiple_of(k_slot * 1024 + inside, BLK)
            v_row = pl.multiple_of(v_slot * 1024 + inside, BLK)
            ksel[t * BLK : (t + 1) * BLK, :] = kv[pl.ds(k_row, BLK), :]
            vsel[t * BLK : (t + 1) * BLK, :] = kv[pl.ds(v_row, BLK), :]
        rows = pl.ds(pl.multiple_of(i * BLK, BLK), BLK)
        cos, sin = cosine[rows, :], sine[rows, :]
        for h in range(heads):
            q = rotated(raw[rows, h * HD : (h + 1) * HD], cos, sin) * HD**-0.5
            qsel[h * BLK : (h + 1) * BLK, :] = q.astype(BF16)
        scores = lax.dot_general(
            ksel[...], qsel[...], (((1,), (1,)), ((), ())), preferred_element_type=F32
        )
        parts = []
        for t in range(PICKS):
            part = scores[t * BLK : (t + 1) * BLK, :]
            if t == 0:
                key = lax.broadcasted_iota(jnp.int32, part.shape, 0)
                query = lax.rem(lax.broadcasted_iota(jnp.int32, part.shape, 1), BLK)
                part = jnp.where(key <= query, part, -1e30)
            else:
                part = part + jnp.where(picks[i, t] > block, -1e30, 0.0).astype(F32)
            parts.append(part)
        scores = jnp.concatenate(parts, axis=0)
        top = jnp.max(scores, axis=0, keepdims=True)
        weights = jnp.exp(scores - top)
        total = jnp.sum(weights, axis=0, keepdims=True)
        mixed = lax.dot_general(
            vsel[...], weights.astype(BF16), (((0,), (0,)), ((), ())), preferred_element_type=F32
        )
        mixed = (mixed / total).T.astype(BF16)
        for h in range(heads):
            out[rows, h * HD : (h + 1) * HD] = mixed[h * BLK : (h + 1) * BLK, :]
        return carry

    lax.fori_loop(0, nblk, body, 0)


def attend(picks, where, raw, cosine, sine, kv):
    rows, width = raw.shape
    heads = width // HD
    nblk = rows // BLK
    smem = pl.BlockSpec(memory_space=pltpu.SMEM)
    vmem = pl.BlockSpec(memory_space=pltpu.VMEM)
    pairs = rows * heads * PICKS * BLK
    return pl.pallas_call(
        functools.partial(attend_kernel, nblk, heads),
        in_specs=[smem, smem, vmem, vmem, vmem, vmem],
        out_specs=vmem,
        out_shape=jax.ShapeDtypeStruct((rows, width), BF16),
        scratch_shapes=[
            pltpu.VMEM((PICKS * BLK, HD), BF16),
            pltpu.VMEM((PICKS * BLK, HD), BF16),
            pltpu.VMEM((heads * BLK, HD), BF16),
        ],
        compiler_params=pltpu.CompilerParams(vmem_limit_bytes=40 << 20),
        cost_estimate=pl.CostEstimate(
            flops=4 * pairs * HD, bytes_accessed=kv.size * 2 + raw.size * 8, transcendentals=pairs
        ),
    )(picks, where, raw, cosine, sine, kv)


def tables_of(first, rows):
    positions = first + jnp.arange(rows)
    half = HD // 2
    freq = 500000.0 ** (-(jnp.arange(half).astype(F32) * 2.0 / HD))
    angle = positions.astype(F32)[:, None] * freq[None, :]
    cosine, sine = jnp.cos(angle), jnp.sin(angle)
    return jnp.concatenate([cosine, cosine], 1), jnp.concatenate([-sine, sine], 1)


def local(activations, query_weight, kv_weight, picks):
    own = activations[0]
    rows = own.shape[0]
    shard = query_weight.shape[0]
    width = query_weight.shape[1] // 2
    dp, seq = lax.axis_index("dp"), lax.axis_index("seq")
    y, z_lo = dp % SIDE, dp // SIDE
    z_hi, x, c = seq // 8, (seq // 2) % SIDE, seq % 2
    step = 1 - 2 * c
    along = step * (1 - 2 * (x % 2))

    def blocks(*names):
        return jnp.stack(
            [(z_lo ^ flip) * SIDE + (y + along * k + SIDE) % SIDE for k, flip in names]
        ).astype(jnp.int32)

    kv_a0 = lax.dynamic_slice(kv_weight, (0, c * HD), (shard, HD))
    sib = get(own, FROM_CORE)
    sib_picks = get(picks[0], FROM_CORE)
    a0 = lax.dynamic_slice(query_weight, (0, c * width), (shard, width))
    kv_a1, kv_b0 = get(kv_a0, FROM_Y), get(kv_a0, FROM_Z)
    kv_a1, kv_b0 = fence((kv_a1, kv_b0))
    kv_a2, kv_b1, kv_a3 = get(kv_a1, FROM_Y), get(kv_a1, FROM_Z), get(kv_a1, FROM_PAIR)
    kv_a2, kv_b1, kv_a3, a0 = fence((kv_a2, kv_b1, kv_a3, a0))
    a1 = get(a0, FROM_Y)
    kv_b2, kv_b3 = get(kv_a2, FROM_Z), get(kv_b1, FROM_PAIR)
    kv_b2, kv_b3, sib, a0 = fence((kv_b2, kv_b3, sib, a0))
    b0 = get(a0, FROM_Z)

    cos_own, sin_own = tables_of(seq * rows, rows)
    cos_sib, sin_sib = tables_of((seq + step) * rows, rows)
    plain = c == 1
    kv_tables = [
        jnp.where(plain, 1.0, cos_own), jnp.where(plain, 0.0, sin_own),
        jnp.where(plain, 1.0, cos_sib), jnp.where(plain, 0.0, sin_sib),
    ]
    kv_own, kv_sib = project(
        blocks(*[(k, flip) for flip in (0, 1) for k in range(SIDE)]),
        own, sib, [kv_a0, kv_a1, kv_a2, kv_a3, kv_b0, kv_b1, kv_b2, kv_b3],
        tables=kv_tables,
    )
    here = jnp.where(
        plain,
        jnp.concatenate([kv_sib, kv_own], 0),
        jnp.concatenate([kv_own, kv_sib], 0),
    )
    here, a1, b0 = fence((here, a1, b0))
    a2 = get(a1, FROM_Y)
    b1 = get(a1, FROM_Z)
    a3 = get(a1, FROM_PAIR)
    near = jnp.concatenate([here, get(here, FROM_Z2)], 0)
    acc = project_query(blocks((0, 0), (1, 0), (0, 1)), own, sib, [a0, a1, b0])
    near, a2, b1, a3, acc = fence((near, a2, b1, a3, acc))
    ahead, back = get(near, FROM_X), get(near, FROM_X_BACK)
    b2 = get(b1, FROM_Y)
    b3 = get(a3, FROM_Z)
    acc = project_query(blocks((2, 0), (3, 0), (1, 1)), own, sib, [a2, a3, b1], acc)
    ahead, back, *acc = fence((ahead, back, *acc))
    chunks = [near, ahead, get(ahead, FROM_X), back]
    kv = jnp.concatenate(chunks + [get(chunk, FROM_CORE) for chunk in chunks], 0)
    acc = project_query(blocks((2, 1), (3, 1)), own, sib, [b2, b3], acc)

    blocks_here = rows // BLK

    def where(s):
        return jnp.stack([s * blocks_here, x, z_hi, c]).astype(jnp.int32)

    out_sib = attend(sib_picks, where(seq + step), acc[1], cos_sib, sin_sib, kv)
    received = get(out_sib, FROM_CORE)
    out_own = attend(picks[0], where(seq), acc[0], cos_own, sin_own, kv)
    out = jnp.where(
        plain,
        jnp.concatenate([received, out_own], 1),
        jnp.concatenate([out_own, received], 1),
    )
    return out[None]


def solution(mesh):
    in_specs = (P("dp", "seq", None), P("dp", None), P("dp", None), P("dp", "seq", None))
    out_specs = P("dp", "seq", None)
    return jax.shard_map(local, mesh=mesh, in_specs=in_specs, out_specs=out_specs, check_vma=False)
```

```python
import functools

import jax
import jax.numpy as jnp
from jax import lax
from jax.experimental import pallas as pl
from jax.experimental.pallas import tpu as pltpu
from jax.sharding import PartitionSpec as P

QH = 8
HD = 128
BLK = 64
PICKS = 16
SIDE = 4
AXES = ("dp", "seq")
F32 = jnp.float32
BF16 = jnp.bfloat16


def place(x, y, z, c):
    x, y, z = x % SIDE, y % SIDE, z % SIDE
    return ((z % 2) * SIDE + y) * 16 + (z // 2) * 8 + x * 2 + c


def receive_from(source):
    r = range(SIDE)
    return [
        (place(*source(x, y, z, c)), place(x, y, z, c))
        for x in r for y in r for z in r for c in range(2)
    ]


def sign(c):
    return 1 - 2 * c


FROM_Y = receive_from(lambda x, y, z, c: (x, y + sign(c) * sign(x % 2), z, c))
FROM_Z = receive_from(lambda x, y, z, c: (x, y, z + sign(c), c))
FROM_X = receive_from(lambda x, y, z, c: (x + sign(c), y, z, c))
FROM_X_BACK = receive_from(lambda x, y, z, c: (x - sign(c), y, z, c))
FROM_Z2 = receive_from(lambda x, y, z, c: (x, y, z + 2, c))
FROM_PAIR = receive_from(lambda x, y, z, c: (x + sign(x % 2) * sign(c), y, z, c))
FROM_CORE = receive_from(lambda x, y, z, c: (x, y, z, 1 - c))


def get(value, perm):
    return lax.ppermute(value, AXES, perm)


fence = lax.optimization_barrier


def rotated(raw, cosine, sine):
    return raw * cosine + pltpu.roll(raw, HD // 2, 1) * sine


def project_kernel(n, first, last, *refs):
    refs = list(refs)
    refs.pop(0)
    own, sib = refs.pop(0), refs.pop(0)
    pieces = [refs.pop(0) for _ in range(n)]
    g = pl.program_id(0)
    if not first:
        acc_own, acc_sib = refs.pop(0), refs.pop(0)
    if last:
        tables = [refs.pop(0) for _ in range(4)]
        fin_own, fin_sib = refs.pop(0), refs.pop(0)
    out_own, out_sib = refs.pop(0), refs.pop(0)
    for p in range(n):

        @pl.when(g == p)
        def _(p=p):
            for x, out, base in (
                (own, out_own, None if first else acc_own),
                (sib, out_sib, None if first else acc_sib),
            ):
                part = jnp.dot(x[...], pieces[p][...], preferred_element_type=F32)
                if p:
                    out[...] += part
                elif first:
                    out[...] = part
                else:
                    out[...] = base[...] + part

    if last:

        @pl.when(g == n - 1)
        def _():
            fin_own[...] = rotated(out_own[...], tables[0][...], tables[1][...]).astype(BF16)
            fin_sib[...] = rotated(out_sib[...], tables[2][...], tables[3][...]).astype(BF16)


def project(blocks, own, sib, pieces, acc=None, tables=None):
    n = len(pieces)
    rows = own.shape[0]
    depth, width = pieces[0].shape
    first, last = acc is None, tables is not None

    def whole(shape):
        return pl.BlockSpec(shape, lambda g, b: (0,) * len(shape))

    tile = pl.BlockSpec((rows, depth), lambda g, b: (0, b[g]))
    in_specs = [tile, tile] + [whole((depth, width))] * n
    args = [own, sib, *pieces]
    if not first:
        in_specs += [whole((rows, width))] * 2
        args += list(acc)
    scratch = []
    if last:
        in_specs += [whole((rows, width))] * 4
        args += list(tables)
        scratch = [pltpu.VMEM((rows, width), F32)] * 2
    return pl.pallas_call(
        functools.partial(project_kernel, n, first, last),
        grid_spec=pltpu.PrefetchScalarGridSpec(
            num_scalar_prefetch=1,
            grid=(n,),
            in_specs=in_specs,
            out_specs=[whole((rows, width))] * 2,
            scratch_shapes=scratch,
        ),
        out_shape=[jax.ShapeDtypeStruct((rows, width), BF16 if last else F32)] * 2,
        compiler_params=pltpu.CompilerParams(vmem_limit_bytes=56 << 20),
        cost_estimate=pl.CostEstimate(
            flops=4 * rows * depth * width * n,
            bytes_accessed=n * depth * (4 * rows + 2 * width) + 16 * rows * width,
            transcendentals=0,
        ),
    )(blocks, *args)


def query_kernel(n, first, blocks, own, sib, *refs):
    pieces, refs = refs[:n], refs[n:]
    bases, (out_own, out_sib, held, sems) = refs[:-4], refs[-4:]
    g = pl.program_id(0)

    def fetch(p):
        return pltpu.make_async_copy(pieces[p], held.at[p % 2], sems.at[p % 2])

    for p in range(n):

        @pl.when(g == p)
        def _(p=p):
            if p == 0:
                fetch(0).start()
            if p + 1 < n:
                fetch(p + 1).start()
            fetch(p).wait()
            for i, (x, out) in enumerate(((own, out_own), (sib, out_sib))):
                part = jnp.dot(x[...], held[p % 2], preferred_element_type=F32)
                if p:
                    out[...] += part
                elif first:
                    out[...] = part
                else:
                    out[...] = bases[i][...] + part


def project_query(blocks, own, sib, pieces, acc=()):
    n = len(pieces)
    rows = own.shape[0]
    depth, width = pieces[0].shape
    tile = pl.BlockSpec((rows, depth), lambda g, b: (0, b[g]))
    result = pl.BlockSpec((rows, width), lambda g, b: (0, 0))
    return pl.pallas_call(
        functools.partial(query_kernel, n, not acc),
        grid_spec=pltpu.PrefetchScalarGridSpec(
            num_scalar_prefetch=1,
            grid=(n,),
            in_specs=[tile, tile]
            + [pl.BlockSpec(memory_space=pl.ANY)] * n
            + [result] * len(acc),
            out_specs=[result] * 2,
            scratch_shapes=[pltpu.VMEM((2, depth, width), BF16), pltpu.SemaphoreType.DMA((2,))],
        ),
        out_shape=[jax.ShapeDtypeStruct((rows, width), F32)] * 2,
        compiler_params=pltpu.CompilerParams(vmem_limit_bytes=40 << 20),
        cost_estimate=pl.CostEstimate(
            flops=4 * rows * depth * width * n,
            bytes_accessed=n * depth * (4 * rows + 2 * width) + 16 * rows * width,
            transcendentals=0,
        ),
    )(blocks, own, sib, *pieces, *acc)


def attend_kernel(nblk, heads, picks, where, raw, cosine, sine, kv, out, ksel, vsel, qsel):
    def body(i, carry):
        block = where[0] + i
        core = where[3]
        for t in range(PICKS):
            pick = picks[i, t]
            chunk = pick // 16
            inside = (pick % 16) * BLK
            away_x = chunk % SIDE - where[1] + SIDE
            away_z = lax.rem(chunk // SIDE + where[2], 2)
            k_slot = lax.rem(away_x, SIDE) * 2 + away_z + core * 8
            v_slot = lax.rem(2 * SIDE - away_x, SIDE) * 2 + away_z + (1 - core) * 8
            k_row = pl.multiple_of(k_slot * 1024 + inside, BLK)
            v_row = pl.multiple_of(v_slot * 1024 + inside, BLK)
            ksel[t * BLK : (t + 1) * BLK, :] = kv[pl.ds(k_row, BLK), :]
            vsel[t * BLK : (t + 1) * BLK, :] = kv[pl.ds(v_row, BLK), :]
        rows = pl.ds(pl.multiple_of(i * BLK, BLK), BLK)
        cos, sin = cosine[rows, :], sine[rows, :]
        for h in range(heads):
            q = rotated(raw[rows, h * HD : (h + 1) * HD], cos, sin) * HD**-0.5
            qsel[h * BLK : (h + 1) * BLK, :] = q.astype(BF16)
        scores = lax.dot_general(
            ksel[...], qsel[...], (((1,), (1,)), ((), ())), preferred_element_type=F32
        )
        parts = []
        for t in range(PICKS):
            part = scores[t * BLK : (t + 1) * BLK, :]
            if t == 0:
                key = lax.broadcasted_iota(jnp.int32, part.shape, 0)
                query = lax.rem(lax.broadcasted_iota(jnp.int32, part.shape, 1), BLK)
                part = jnp.where(key <= query, part, -1e30)
            else:
                part = part + jnp.where(picks[i, t] > block, -1e30, 0.0).astype(F32)
            parts.append(part)
        scores = jnp.concatenate(parts, axis=0)
        top = jnp.max(scores, axis=0, keepdims=True)
        weights = jnp.exp(scores - top)
        total = jnp.sum(weights, axis=0, keepdims=True)
        mixed = lax.dot_general(
            vsel[...], weights.astype(BF16), (((0,), (0,)), ((), ())), preferred_element_type=F32
        )
        mixed = (mixed / total).T.astype(BF16)
        for h in range(heads):
            out[rows, h * HD : (h + 1) * HD] = mixed[h * BLK : (h + 1) * BLK, :]
        return carry

    lax.fori_loop(0, nblk, body, 0)


def attend(picks, where, raw, cosine, sine, kv):
    rows, width = raw.shape
    heads = width // HD
    nblk = rows // BLK
    smem = pl.BlockSpec(memory_space=pltpu.SMEM)
    vmem = pl.BlockSpec(memory_space=pltpu.VMEM)
    pairs = rows * heads * PICKS * BLK
    return pl.pallas_call(
        functools.partial(attend_kernel, nblk, heads),
        in_specs=[smem, smem, vmem, vmem, vmem, vmem],
        out_specs=vmem,
        out_shape=jax.ShapeDtypeStruct((rows, width), BF16),
        scratch_shapes=[
            pltpu.VMEM((PICKS * BLK, HD), BF16),
            pltpu.VMEM((PICKS * BLK, HD), BF16),
            pltpu.VMEM((heads * BLK, HD), BF16),
        ],
        compiler_params=pltpu.CompilerParams(vmem_limit_bytes=40 << 20),
        cost_estimate=pl.CostEstimate(
            flops=4 * pairs * HD, bytes_accessed=kv.size * 2 + raw.size * 8, transcendentals=pairs
        ),
    )(picks, where, raw, cosine, sine, kv)


def tables_of(first, rows):
    positions = first + jnp.arange(rows)
    half = HD // 2
    freq = 500000.0 ** (-(jnp.arange(half).astype(F32) * 2.0 / HD))
    angle = positions.astype(F32)[:, None] * freq[None, :]
    cosine, sine = jnp.cos(angle), jnp.sin(angle)
    return jnp.concatenate([cosine, cosine], 1), jnp.concatenate([-sine, sine], 1)


def local(activations, query_weight, kv_weight, picks):
    own = activations[0]
    rows = own.shape[0]
    shard = query_weight.shape[0]
    width = query_weight.shape[1] // 2
    dp, seq = lax.axis_index("dp"), lax.axis_index("seq")
    y, z_lo = dp % SIDE, dp // SIDE
    z_hi, x, c = seq // 8, (seq // 2) % SIDE, seq % 2
    step = 1 - 2 * c
    along = step * (1 - 2 * (x % 2))

    def blocks(*names):
        return jnp.stack(
            [(z_lo ^ flip) * SIDE + (y + along * k + SIDE) % SIDE for k, flip in names]
        ).astype(jnp.int32)

    kv_a0 = lax.dynamic_slice(kv_weight, (0, c * HD), (shard, HD))
    sib = get(own, FROM_CORE)
    sib_picks = get(picks[0], FROM_CORE)
    a0 = lax.dynamic_slice(query_weight, (0, c * width), (shard, width))
    kv_a1, kv_b0 = get(kv_a0, FROM_Y), get(kv_a0, FROM_Z)
    cos_own, sin_own = tables_of(seq * rows, rows)
    cos_sib, sin_sib = tables_of((seq + step) * rows, rows)
    plain = c == 1
    kv_tables = [
        jnp.where(plain, 1.0, cos_own), jnp.where(plain, 0.0, sin_own),
        jnp.where(plain, 1.0, cos_sib), jnp.where(plain, 0.0, sin_sib),
    ]
    kv_a1, kv_b0, cos_own, sin_own, cos_sib, sin_sib, kv_tables = fence(
        (kv_a1, kv_b0, cos_own, sin_own, cos_sib, sin_sib, kv_tables)
    )
    kv_a2, kv_b1, kv_a3 = get(kv_a1, FROM_Y), get(kv_a1, FROM_Z), get(kv_a1, FROM_PAIR)
    kv_a2, kv_b1, kv_a3, a0 = fence((kv_a2, kv_b1, kv_a3, a0))
    a1 = get(a0, FROM_Y)
    kv_b2, kv_b3 = get(kv_a2, FROM_Z), get(kv_b1, FROM_PAIR)
    kv_b2, kv_b3, sib, a0 = fence((kv_b2, kv_b3, sib, a0))
    b0 = get(a0, FROM_Z)

    acc = project(
        blocks((0, 0), (1, 0), (2, 0), (3, 0)), own, sib, [kv_a0, kv_a1, kv_a2, kv_a3]
    )
    kv_b0, a1, *acc = fence((kv_b0, a1, *acc))
    a2 = get(a1, FROM_Y)
    b1 = get(a1, FROM_Z)
    a3 = get(a1, FROM_PAIR)
    kv_own, kv_sib = project(
        blocks((0, 1), (1, 1), (2, 1), (3, 1)),
        own, sib, [kv_b0, kv_b1, kv_b2, kv_b3], acc, tables=kv_tables,
    )
    here = jnp.where(
        plain,
        jnp.concatenate([kv_sib, kv_own], 0),
        jnp.concatenate([kv_own, kv_sib], 0),
    )
    here, b0 = fence((here, b0))
    near = jnp.concatenate([here, get(here, FROM_Z2)], 0)
    acc = project_query(blocks((0, 0), (1, 0), (0, 1)), own, sib, [a0, a1, b0])
    a2, b1, a3, acc = fence((a2, b1, a3, acc))
    b2 = get(b1, FROM_Y)
    b3 = get(a3, FROM_Z)
    near, a2, acc = fence((near, a2, acc))
    ahead, back = get(near, FROM_X), get(near, FROM_X_BACK)
    acc = project_query(blocks((2, 0), (3, 0), (1, 1)), own, sib, [a2, a3, b1], acc)
    ahead, back, *acc = fence((ahead, back, *acc))
    chunks = [near, ahead, get(ahead, FROM_X), back]
    kv = jnp.concatenate(chunks + [get(chunk, FROM_CORE) for chunk in chunks], 0)
    acc = project_query(blocks((2, 1), (3, 1)), own, sib, [b2, b3], acc)

    blocks_here = rows // BLK

    def where(s):
        return jnp.stack([s * blocks_here, x, z_hi, c]).astype(jnp.int32)

    out_sib = attend(sib_picks, where(seq + step), acc[1], cos_sib, sin_sib, kv)
    received = get(out_sib, FROM_CORE)
    out_own = attend(picks[0], where(seq), acc[0], cos_own, sin_own, kv)
    out = jnp.where(
        plain,
        jnp.concatenate([received, out_own], 1),
        jnp.concatenate([out_own, received], 1),
    )
    return out[None]


def solution(mesh):
    in_specs = (P("dp", "seq", None), P("dp", None), P("dp", None), P("dp", "seq", None))
    out_specs = P("dp", "seq", None)
    return jax.shard_map(local, mesh=mesh, in_specs=in_specs, out_specs=out_specs, check_vma=False)
```

```python
import functools

import jax
import jax.numpy as jnp
from jax import lax
from jax.experimental import pallas as pl
from jax.experimental.pallas import tpu as pltpu
from jax.sharding import PartitionSpec as P

QH = 8
HD = 128
BLK = 64
PICKS = 16
SIDE = 4
AXES = ("dp", "seq")
F32 = jnp.float32
BF16 = jnp.bfloat16


def place(x, y, z, c):
    x, y, z = x % SIDE, y % SIDE, z % SIDE
    return ((z % 2) * SIDE + y) * 16 + (z // 2) * 8 + x * 2 + c


def receive_from(source):
    r = range(SIDE)
    return [
        (place(*source(x, y, z, c)), place(x, y, z, c))
        for x in r for y in r for z in r for c in range(2)
    ]


def sign(c):
    return 1 - 2 * c


FROM_Y = receive_from(lambda x, y, z, c: (x, y + sign(c) * sign(x % 2), z, c))
FROM_Z = receive_from(lambda x, y, z, c: (x, y, z + sign(c), c))
FROM_X = receive_from(lambda x, y, z, c: (x + sign(c), y, z, c))
FROM_X_BACK = receive_from(lambda x, y, z, c: (x - sign(c), y, z, c))
FROM_Z2 = receive_from(lambda x, y, z, c: (x, y, z + 2, c))
FROM_PAIR = receive_from(lambda x, y, z, c: (x + sign(x % 2) * sign(c), y, z, c))
FROM_CORE = receive_from(lambda x, y, z, c: (x, y, z, 1 - c))


def get(value, perm):
    return lax.ppermute(value, AXES, perm)


fence = lax.optimization_barrier


def rotated(raw, cosine, sine):
    return raw * cosine + pltpu.roll(raw, HD // 2, 1) * sine


def project_kernel(n, first, last, *refs):
    refs = list(refs)
    refs.pop(0)
    own, sib = refs.pop(0), refs.pop(0)
    pieces = [refs.pop(0) for _ in range(n)]
    g = pl.program_id(0)
    if not first:
        acc_own, acc_sib = refs.pop(0), refs.pop(0)
    if last:
        tables = [refs.pop(0) for _ in range(4)]
        fin_own, fin_sib = refs.pop(0), refs.pop(0)
    out_own, out_sib = refs.pop(0), refs.pop(0)
    for p in range(n):

        @pl.when(g == p)
        def _(p=p):
            for x, out, base in (
                (own, out_own, None if first else acc_own),
                (sib, out_sib, None if first else acc_sib),
            ):
                part = jnp.dot(x[...], pieces[p][...], preferred_element_type=F32)
                if p:
                    out[...] += part
                elif first:
                    out[...] = part
                else:
                    out[...] = base[...] + part

    if last:

        @pl.when(g == n - 1)
        def _():
            fin_own[...] = rotated(out_own[...], tables[0][...], tables[1][...]).astype(BF16)
            fin_sib[...] = rotated(out_sib[...], tables[2][...], tables[3][...]).astype(BF16)


def project(blocks, own, sib, pieces, acc=None, tables=None):
    n = len(pieces)
    rows = own.shape[0]
    depth, width = pieces[0].shape
    first, last = acc is None, tables is not None

    def whole(shape):
        return pl.BlockSpec(shape, lambda g, b: (0,) * len(shape))

    tile = pl.BlockSpec((rows, depth), lambda g, b: (0, b[g]))
    in_specs = [tile, tile] + [whole((depth, width))] * n
    args = [own, sib, *pieces]
    if not first:
        in_specs += [whole((rows, width))] * 2
        args += list(acc)
    scratch = []
    if last:
        in_specs += [whole((rows, width))] * 4
        args += list(tables)
        scratch = [pltpu.VMEM((rows, width), F32)] * 2
    return pl.pallas_call(
        functools.partial(project_kernel, n, first, last),
        grid_spec=pltpu.PrefetchScalarGridSpec(
            num_scalar_prefetch=1,
            grid=(n,),
            in_specs=in_specs,
            out_specs=[whole((rows, width))] * 2,
            scratch_shapes=scratch,
        ),
        out_shape=[jax.ShapeDtypeStruct((rows, width), BF16 if last else F32)] * 2,
        compiler_params=pltpu.CompilerParams(vmem_limit_bytes=56 << 20),
        cost_estimate=pl.CostEstimate(
            flops=4 * rows * depth * width * n,
            bytes_accessed=n * depth * (4 * rows + 2 * width) + 16 * rows * width,
            transcendentals=0,
        ),
    )(blocks, *args)


def query_kernel(n, first, blocks, own, sib, *refs):
    pieces, refs = refs[:n], refs[n:]
    bases, (out_own, out_sib, held, sems) = refs[:-4], refs[-4:]
    g = pl.program_id(0)

    def fetch(p):
        return pltpu.make_async_copy(pieces[p], held.at[p % 2], sems.at[p % 2])

    for p in range(n):

        @pl.when(g == p)
        def _(p=p):
            if p == 0:
                fetch(0).start()
            if p + 1 < n:
                fetch(p + 1).start()
            fetch(p).wait()
            for i, (x, out) in enumerate(((own, out_own), (sib, out_sib))):
                part = jnp.dot(x[...], held[p % 2], preferred_element_type=F32)
                if p:
                    out[...] += part
                elif first:
                    out[...] = part
                else:
                    out[...] = bases[i][...] + part


def project_query(blocks, own, sib, pieces, acc=()):
    n = len(pieces)
    rows = own.shape[0]
    depth, width = pieces[0].shape
    tile = pl.BlockSpec((rows, depth), lambda g, b: (0, b[g]))
    result = pl.BlockSpec((rows, width), lambda g, b: (0, 0))
    return pl.pallas_call(
        functools.partial(query_kernel, n, not acc),
        grid_spec=pltpu.PrefetchScalarGridSpec(
            num_scalar_prefetch=1,
            grid=(n,),
            in_specs=[tile, tile]
            + [pl.BlockSpec(memory_space=pl.ANY)] * n
            + [result] * len(acc),
            out_specs=[result] * 2,
            scratch_shapes=[pltpu.VMEM((2, depth, width), BF16), pltpu.SemaphoreType.DMA((2,))],
        ),
        out_shape=[jax.ShapeDtypeStruct((rows, width), F32)] * 2,
        compiler_params=pltpu.CompilerParams(vmem_limit_bytes=40 << 20),
        cost_estimate=pl.CostEstimate(
            flops=4 * rows * depth * width * n,
            bytes_accessed=n * depth * (4 * rows + 2 * width) + 16 * rows * width,
            transcendentals=0,
        ),
    )(blocks, own, sib, *pieces, *acc)


def attend_kernel(nblk, heads, picks, where, raw, cosine, sine, kv, out, ksel, vsel, qsel):
    def body(i, carry):
        block = where[0] + i
        core = where[3]
        for t in range(PICKS):
            pick = picks[i, t]
            chunk = pick // 16
            inside = (pick % 16) * BLK
            away_x = chunk % SIDE - where[1] + SIDE
            away_z = lax.rem(chunk // SIDE + where[2], 2)
            k_slot = lax.rem(away_x, SIDE) * 2 + away_z + core * 8
            v_slot = lax.rem(2 * SIDE - away_x, SIDE) * 2 + away_z + (1 - core) * 8
            k_row = pl.multiple_of(k_slot * 1024 + inside, BLK)
            v_row = pl.multiple_of(v_slot * 1024 + inside, BLK)
            ksel[t * BLK : (t + 1) * BLK, :] = kv[pl.ds(k_row, BLK), :]
            vsel[t * BLK : (t + 1) * BLK, :] = kv[pl.ds(v_row, BLK), :]
        rows = pl.ds(pl.multiple_of(i * BLK, BLK), BLK)
        cos, sin = cosine[rows, :], sine[rows, :]
        for h in range(heads):
            q = rotated(raw[rows, h * HD : (h + 1) * HD], cos, sin) * HD**-0.5
            qsel[h * BLK : (h + 1) * BLK, :] = q.astype(BF16)
        scores = lax.dot_general(
            ksel[...], qsel[...], (((1,), (1,)), ((), ())), preferred_element_type=F32
        )
        parts = []
        for t in range(PICKS):
            part = scores[t * BLK : (t + 1) * BLK, :]
            if t == 0:
                key = lax.broadcasted_iota(jnp.int32, part.shape, 0)
                query = lax.rem(lax.broadcasted_iota(jnp.int32, part.shape, 1), BLK)
                part = jnp.where(key <= query, part, -1e30)
            else:
                part = part + jnp.where(picks[i, t] > block, -1e30, 0.0).astype(F32)
            parts.append(part)
        scores = jnp.concatenate(parts, axis=0)
        top = jnp.max(scores, axis=0, keepdims=True)
        weights = jnp.exp(scores - top)
        total = jnp.sum(weights, axis=0, keepdims=True)
        mixed = lax.dot_general(
            vsel[...], weights.astype(BF16), (((0,), (0,)), ((), ())), preferred_element_type=F32
        )
        mixed = (mixed / total).T.astype(BF16)
        for h in range(heads):
            out[rows, h * HD : (h + 1) * HD] = mixed[h * BLK : (h + 1) * BLK, :]
        return carry

    lax.fori_loop(0, nblk, body, 0)


def attend(picks, where, raw, cosine, sine, kv, limit):
    rows, width = raw.shape
    heads = width // HD
    nblk = rows // BLK
    smem = pl.BlockSpec(memory_space=pltpu.SMEM)
    vmem = pl.BlockSpec(memory_space=pltpu.VMEM)
    pairs = rows * heads * PICKS * BLK
    return pl.pallas_call(
        functools.partial(attend_kernel, nblk, heads),
        in_specs=[smem, smem, vmem, vmem, vmem, vmem],
        out_specs=vmem,
        out_shape=jax.ShapeDtypeStruct((rows, width), BF16),
        scratch_shapes=[
            pltpu.VMEM((PICKS * BLK, HD), BF16),
            pltpu.VMEM((PICKS * BLK, HD), BF16),
            pltpu.VMEM((heads * BLK, HD), BF16),
        ],
        compiler_params=pltpu.CompilerParams(vmem_limit_bytes=limit << 20),
        cost_estimate=pl.CostEstimate(
            flops=4 * pairs * HD, bytes_accessed=kv.size * 2 + raw.size * 8, transcendentals=pairs
        ),
    )(picks, where, raw, cosine, sine, kv)


def tables_of(first, rows):
    positions = first + jnp.arange(rows)
    half = HD // 2
    freq = 500000.0 ** (-(jnp.arange(half).astype(F32) * 2.0 / HD))
    angle = positions.astype(F32)[:, None] * freq[None, :]
    cosine, sine = jnp.cos(angle), jnp.sin(angle)
    return jnp.concatenate([cosine, cosine], 1), jnp.concatenate([-sine, sine], 1)


def local(activations, query_weight, kv_weight, picks):
    own = activations[0]
    rows = own.shape[0]
    shard = query_weight.shape[0]
    width = query_weight.shape[1] // 2
    dp, seq = lax.axis_index("dp"), lax.axis_index("seq")
    y, z_lo = dp % SIDE, dp // SIDE
    z_hi, x, c = seq // 8, (seq // 2) % SIDE, seq % 2
    step = 1 - 2 * c
    along = step * (1 - 2 * (x % 2))

    def blocks(*names):
        return jnp.stack(
            [(z_lo ^ flip) * SIDE + (y + along * k + SIDE) % SIDE for k, flip in names]
        ).astype(jnp.int32)

    kv_a0 = lax.dynamic_slice(kv_weight, (0, c * HD), (shard, HD))
    sib = get(own, FROM_CORE)
    sib_picks = get(picks[0], FROM_CORE)
    a0 = lax.dynamic_slice(query_weight, (0, c * width), (shard, width))
    kv_a1, kv_b0 = get(kv_a0, FROM_Y), get(kv_a0, FROM_Z)
    cos_own, sin_own = tables_of(seq * rows, rows)
    cos_sib, sin_sib = tables_of((seq + step) * rows, rows)
    plain = c == 1
    kv_tables = [
        jnp.where(plain, 1.0, cos_own), jnp.where(plain, 0.0, sin_own),
        jnp.where(plain, 1.0, cos_sib), jnp.where(plain, 0.0, sin_sib),
    ]
    kv_a1, kv_b0, cos_own, sin_own, cos_sib, sin_sib, kv_tables = fence(
        (kv_a1, kv_b0, cos_own, sin_own, cos_sib, sin_sib, kv_tables)
    )
    kv_a2, kv_b1, kv_a3 = get(kv_a1, FROM_Y), get(kv_a1, FROM_Z), get(kv_a1, FROM_PAIR)
    kv_a2, kv_b1, kv_a3, a0 = fence((kv_a2, kv_b1, kv_a3, a0))
    a1 = get(a0, FROM_Y)
    kv_b2, kv_b3 = get(kv_a2, FROM_Z), get(kv_b1, FROM_PAIR)
    kv_b2, kv_b3, sib, a0 = fence((kv_b2, kv_b3, sib, a0))
    b0 = get(a0, FROM_Z)

    acc = project(
        blocks((0, 0), (1, 0), (2, 0), (3, 0)), own, sib, [kv_a0, kv_a1, kv_a2, kv_a3]
    )
    kv_b0, a1, *acc = fence((kv_b0, a1, *acc))
    a2 = get(a1, FROM_Y)
    b1 = get(a1, FROM_Z)
    a3 = get(a1, FROM_PAIR)
    kv_own, kv_sib = project(
        blocks((0, 1), (1, 1), (2, 1), (3, 1)),
        own, sib, [kv_b0, kv_b1, kv_b2, kv_b3], acc, tables=kv_tables,
    )
    here = jnp.where(
        plain,
        jnp.concatenate([kv_sib, kv_own], 0),
        jnp.concatenate([kv_own, kv_sib], 0),
    )
    here, b0 = fence((here, b0))
    near = jnp.concatenate([here, get(here, FROM_Z2)], 0)
    acc = project_query(blocks((0, 0), (1, 0), (0, 1)), own, sib, [a0, a1, b0])
    a2, b1, a3, acc = fence((a2, b1, a3, acc))
    b2 = get(b1, FROM_Y)
    b3 = get(a3, FROM_Z)
    near, a2, acc = fence((near, a2, acc))
    ahead, back = get(near, FROM_X), get(near, FROM_X_BACK)
    acc = project_query(blocks((2, 0), (3, 0), (1, 1)), own, sib, [a2, a3, b1], acc)
    ahead, back, *acc = fence((ahead, back, *acc))
    chunks = [near, ahead, get(ahead, FROM_X), back]
    kv = jnp.concatenate(chunks + [get(chunk, FROM_CORE) for chunk in chunks], 0)
    acc = project_query(blocks((2, 1), (3, 1)), own, sib, [b2, b3], acc)

    blocks_here = rows // BLK

    def where(s):
        return jnp.stack([s * blocks_here, x, z_hi, c]).astype(jnp.int32)

    out_sib = attend(sib_picks, where(seq + step), acc[1], cos_sib, sin_sib, kv, 40)
    received = get(out_sib, FROM_CORE)
    out_own = attend(picks[0], where(seq), acc[0], cos_own, sin_own, kv, 58)
    out = jnp.where(
        plain,
        jnp.concatenate([received, out_own], 1),
        jnp.concatenate([out_own, received], 1),
    )
    return out[None]


def solution(mesh):
    in_specs = (P("dp", "seq", None), P("dp", None), P("dp", None), P("dp", "seq", None))
    out_specs = P("dp", "seq", None)
    return jax.shard_map(local, mesh=mesh, in_specs=in_specs, out_specs=out_specs, check_vma=False)
```

```python
import functools

import jax
import jax.numpy as jnp
from jax import lax
from jax.experimental import pallas as pl
from jax.experimental.pallas import tpu as pltpu
from jax.sharding import PartitionSpec as P

QH = 8
HD = 128
BLK = 64
PICKS = 16
SIDE = 4
AXES = ("dp", "seq")
F32 = jnp.float32
BF16 = jnp.bfloat16


def place(x, y, z, c):
    x, y, z = x % SIDE, y % SIDE, z % SIDE
    return ((z % 2) * SIDE + y) * 16 + (z // 2) * 8 + x * 2 + c


def receive_from(source):
    r = range(SIDE)
    return [
        (place(*source(x, y, z, c)), place(x, y, z, c))
        for x in r for y in r for z in r for c in range(2)
    ]


def sign(c):
    return 1 - 2 * c


FROM_Y = receive_from(lambda x, y, z, c: (x, y + sign(c) * sign(x % 2), z, c))
FROM_Z = receive_from(lambda x, y, z, c: (x, y, z + sign(c), c))
FROM_X = receive_from(lambda x, y, z, c: (x + sign(c), y, z, c))
FROM_X_BACK = receive_from(lambda x, y, z, c: (x - sign(c), y, z, c))
FROM_Z2 = receive_from(lambda x, y, z, c: (x, y, z + 2, c))
FROM_PAIR = receive_from(lambda x, y, z, c: (x + sign(x % 2) * sign(c), y, z, c))
FROM_CORE = receive_from(lambda x, y, z, c: (x, y, z, 1 - c))


def get(value, perm):
    return lax.ppermute(value, AXES, perm)


fence = lax.optimization_barrier


def rotated(raw, cosine, sine):
    return raw * cosine + pltpu.roll(raw, HD // 2, 1) * sine


def project_kernel(n, first, last, *refs):
    refs = list(refs)
    refs.pop(0)
    own, sib = refs.pop(0), refs.pop(0)
    pieces = [refs.pop(0) for _ in range(n)]
    g = pl.program_id(0)
    if not first:
        acc_own, acc_sib = refs.pop(0), refs.pop(0)
    if last:
        tables = [refs.pop(0) for _ in range(4)]
        fin_own, fin_sib = refs.pop(0), refs.pop(0)
    out_own, out_sib = refs.pop(0), refs.pop(0)
    for p in range(n):

        @pl.when(g == p)
        def _(p=p):
            for x, out, base in (
                (own, out_own, None if first else acc_own),
                (sib, out_sib, None if first else acc_sib),
            ):
                part = jnp.dot(x[...], pieces[p][...], preferred_element_type=F32)
                if p:
                    out[...] += part
                elif first:
                    out[...] = part
                else:
                    out[...] = base[...] + part

    if last:

        @pl.when(g == n - 1)
        def _():
            fin_own[...] = rotated(out_own[...], tables[0][...], tables[1][...]).astype(BF16)
            fin_sib[...] = rotated(out_sib[...], tables[2][...], tables[3][...]).astype(BF16)


def project(blocks, own, sib, pieces, acc=None, tables=None):
    n = len(pieces)
    rows = own.shape[0]
    depth, width = pieces[0].shape
    first, last = acc is None, tables is not None

    def whole(shape):
        return pl.BlockSpec(shape, lambda g, b: (0,) * len(shape))

    tile = pl.BlockSpec((rows, depth), lambda g, b: (0, b[g]))
    in_specs = [tile, tile] + [whole((depth, width))] * n
    args = [own, sib, *pieces]
    if not first:
        in_specs += [whole((rows, width))] * 2
        args += list(acc)
    scratch = []
    if last:
        in_specs += [whole((rows, width))] * 4
        args += list(tables)
        scratch = [pltpu.VMEM((rows, width), F32)] * 2
    return pl.pallas_call(
        functools.partial(project_kernel, n, first, last),
        grid_spec=pltpu.PrefetchScalarGridSpec(
            num_scalar_prefetch=1,
            grid=(n,),
            in_specs=in_specs,
            out_specs=[whole((rows, width))] * 2,
            scratch_shapes=scratch,
        ),
        out_shape=[jax.ShapeDtypeStruct((rows, width), BF16 if last else F32)] * 2,
        compiler_params=pltpu.CompilerParams(vmem_limit_bytes=56 << 20),
        cost_estimate=pl.CostEstimate(
            flops=4 * rows * depth * width * n,
            bytes_accessed=n * depth * (4 * rows + 2 * width) + 16 * rows * width,
            transcendentals=0,
        ),
    )(blocks, *args)


def query_kernel(n, first, blocks, own, sib, *refs):
    pieces, refs = refs[:n], refs[n:]
    bases, (out_own, out_sib, held, sems) = refs[:-4], refs[-4:]
    g = pl.program_id(0)

    def fetch(p):
        return pltpu.make_async_copy(pieces[p], held.at[p % 2], sems.at[p % 2])

    for p in range(n):

        @pl.when(g == p)
        def _(p=p):
            if p == 0:
                fetch(0).start()
            if p + 1 < n:
                fetch(p + 1).start()
            fetch(p).wait()
            for i, (x, out) in enumerate(((own, out_own), (sib, out_sib))):
                part = jnp.dot(x[...], held[p % 2], preferred_element_type=F32)
                if p:
                    out[...] += part
                elif first:
                    out[...] = part
                else:
                    out[...] = bases[i][...] + part


def project_query(blocks, own, sib, pieces, acc=()):
    n = len(pieces)
    rows = own.shape[0]
    depth, width = pieces[0].shape
    tile = pl.BlockSpec((rows, depth), lambda g, b: (0, b[g]))
    result = pl.BlockSpec((rows, width), lambda g, b: (0, 0))
    return pl.pallas_call(
        functools.partial(query_kernel, n, not acc),
        grid_spec=pltpu.PrefetchScalarGridSpec(
            num_scalar_prefetch=1,
            grid=(n,),
            in_specs=[tile, tile]
            + [pl.BlockSpec(memory_space=pl.ANY)] * n
            + [result] * len(acc),
            out_specs=[result] * 2,
            scratch_shapes=[pltpu.VMEM((2, depth, width), BF16), pltpu.SemaphoreType.DMA((2,))],
        ),
        out_shape=[jax.ShapeDtypeStruct((rows, width), F32)] * 2,
        compiler_params=pltpu.CompilerParams(vmem_limit_bytes=40 << 20),
        cost_estimate=pl.CostEstimate(
            flops=4 * rows * depth * width * n,
            bytes_accessed=n * depth * (4 * rows + 2 * width) + 16 * rows * width,
            transcendentals=0,
        ),
    )(blocks, own, sib, *pieces, *acc)


def attend_kernel(nblk, heads, picks, where, raw, cosine, sine, kv, out, ksel, vsel, qsel):
    def body(i, carry):
        block = where[0] + i
        core = where[3]
        for t in range(PICKS):
            pick = picks[i, t]
            chunk = pick // 16
            inside = (pick % 16) * BLK
            away_x = chunk % SIDE - where[1] + SIDE
            away_z = lax.rem(chunk // SIDE + where[2], 2)
            k_slot = lax.rem(away_x, SIDE) * 2 + away_z + core * 8
            v_slot = lax.rem(2 * SIDE - away_x, SIDE) * 2 + away_z + (1 - core) * 8
            k_row = pl.multiple_of(k_slot * 1024 + inside, BLK)
            v_row = pl.multiple_of(v_slot * 1024 + inside, BLK)
            ksel[t * BLK : (t + 1) * BLK, :] = kv[pl.ds(k_row, BLK), :]
            vsel[t * BLK : (t + 1) * BLK, :] = kv[pl.ds(v_row, BLK), :]
        rows = pl.ds(pl.multiple_of(i * BLK, BLK), BLK)
        cos, sin = cosine[rows, :], sine[rows, :]
        for h in range(heads):
            q = rotated(raw[rows, h * HD : (h + 1) * HD], cos, sin) * HD**-0.5
            qsel[h * BLK : (h + 1) * BLK, :] = q.astype(BF16)
        scores = lax.dot_general(
            ksel[...], qsel[...], (((1,), (1,)), ((), ())), preferred_element_type=F32
        )
        parts = []
        for t in range(PICKS):
            part = scores[t * BLK : (t + 1) * BLK, :]
            if t == 0:
                key = lax.broadcasted_iota(jnp.int32, part.shape, 0)
                query = lax.rem(lax.broadcasted_iota(jnp.int32, part.shape, 1), BLK)
                part = jnp.where(key <= query, part, -1e30)
            else:
                part = part + jnp.where(picks[i, t] > block, -1e30, 0.0).astype(F32)
            parts.append(part)
        scores = jnp.concatenate(parts, axis=0)
        top = jnp.max(scores, axis=0, keepdims=True)
        weights = jnp.exp(scores - top)
        total = jnp.sum(weights, axis=0, keepdims=True)
        mixed = lax.dot_general(
            vsel[...], weights.astype(BF16), (((0,), (0,)), ((), ())), preferred_element_type=F32
        )
        mixed = (mixed / total).T.astype(BF16)
        for h in range(heads):
            out[rows, h * HD : (h + 1) * HD] = mixed[h * BLK : (h + 1) * BLK, :]
        return carry

    lax.fori_loop(0, nblk, body, 0, unroll=2)


def attend(picks, where, raw, cosine, sine, kv, limit):
    rows, width = raw.shape
    heads = width // HD
    nblk = rows // BLK
    smem = pl.BlockSpec(memory_space=pltpu.SMEM)
    vmem = pl.BlockSpec(memory_space=pltpu.VMEM)
    pairs = rows * heads * PICKS * BLK
    return pl.pallas_call(
        functools.partial(attend_kernel, nblk, heads),
        in_specs=[smem, smem, vmem, vmem, vmem, vmem],
        out_specs=vmem,
        out_shape=jax.ShapeDtypeStruct((rows, width), BF16),
        scratch_shapes=[
            pltpu.VMEM((PICKS * BLK, HD), BF16),
            pltpu.VMEM((PICKS * BLK, HD), BF16),
            pltpu.VMEM((heads * BLK, HD), BF16),
        ],
        compiler_params=pltpu.CompilerParams(vmem_limit_bytes=limit << 20),
        cost_estimate=pl.CostEstimate(
            flops=4 * pairs * HD, bytes_accessed=kv.size * 2 + raw.size * 8, transcendentals=pairs
        ),
    )(picks, where, raw, cosine, sine, kv)


def tables_of(first, rows):
    positions = first + jnp.arange(rows)
    half = HD // 2
    freq = 500000.0 ** (-(jnp.arange(half).astype(F32) * 2.0 / HD))
    angle = positions.astype(F32)[:, None] * freq[None, :]
    cosine, sine = jnp.cos(angle), jnp.sin(angle)
    return jnp.concatenate([cosine, cosine], 1), jnp.concatenate([-sine, sine], 1)


def local(activations, query_weight, kv_weight, picks):
    own = activations[0]
    rows = own.shape[0]
    shard = query_weight.shape[0]
    width = query_weight.shape[1] // 2
    dp, seq = lax.axis_index("dp"), lax.axis_index("seq")
    y, z_lo = dp % SIDE, dp // SIDE
    z_hi, x, c = seq // 8, (seq // 2) % SIDE, seq % 2
    step = 1 - 2 * c
    along = step * (1 - 2 * (x % 2))

    def blocks(*names):
        return jnp.stack(
            [(z_lo ^ flip) * SIDE + (y + along * k + SIDE) % SIDE for k, flip in names]
        ).astype(jnp.int32)

    kv_a0 = lax.dynamic_slice(kv_weight, (0, c * HD), (shard, HD))
    sib = get(own, FROM_CORE)
    sib_picks = get(picks[0], FROM_CORE)
    a0 = lax.dynamic_slice(query_weight, (0, c * width), (shard, width))
    kv_a1, kv_b0 = get(kv_a0, FROM_Y), get(kv_a0, FROM_Z)
    cos_own, sin_own = tables_of(seq * rows, rows)
    cos_sib, sin_sib = tables_of((seq + step) * rows, rows)
    plain = c == 1
    kv_tables = [
        jnp.where(plain, 1.0, cos_own), jnp.where(plain, 0.0, sin_own),
        jnp.where(plain, 1.0, cos_sib), jnp.where(plain, 0.0, sin_sib),
    ]
    kv_a1, kv_b0, cos_own, sin_own, cos_sib, sin_sib, kv_tables = fence(
        (kv_a1, kv_b0, cos_own, sin_own, cos_sib, sin_sib, kv_tables)
    )
    kv_a2, kv_b1, kv_a3 = get(kv_a1, FROM_Y), get(kv_a1, FROM_Z), get(kv_a1, FROM_PAIR)
    kv_a2, kv_b1, kv_a3, a0 = fence((kv_a2, kv_b1, kv_a3, a0))
    a1 = get(a0, FROM_Y)
    kv_b2, kv_b3 = get(kv_a2, FROM_Z), get(kv_b1, FROM_PAIR)
    kv_b2, kv_b3, sib, a0 = fence((kv_b2, kv_b3, sib, a0))
    b0 = get(a0, FROM_Z)

    acc = project(
        blocks((0, 0), (1, 0), (2, 0), (3, 0)), own, sib, [kv_a0, kv_a1, kv_a2, kv_a3]
    )
    kv_b0, a1, *acc = fence((kv_b0, a1, *acc))
    a2 = get(a1, FROM_Y)
    b1 = get(a1, FROM_Z)
    a3 = get(a1, FROM_PAIR)
    kv_own, kv_sib = project(
        blocks((0, 1), (1, 1), (2, 1), (3, 1)),
        own, sib, [kv_b0, kv_b1, kv_b2, kv_b3], acc, tables=kv_tables,
    )
    here = jnp.where(
        plain,
        jnp.concatenate([kv_sib, kv_own], 0),
        jnp.concatenate([kv_own, kv_sib], 0),
    )
    here, b0 = fence((here, b0))
    near = jnp.concatenate([here, get(here, FROM_Z2)], 0)
    acc = project_query(blocks((0, 0), (1, 0), (0, 1)), own, sib, [a0, a1, b0])
    a2, b1, a3, acc = fence((a2, b1, a3, acc))
    b2 = get(b1, FROM_Y)
    b3 = get(a3, FROM_Z)
    near, a2, acc = fence((near, a2, acc))
    ahead, back = get(near, FROM_X), get(near, FROM_X_BACK)
    acc = project_query(blocks((2, 0), (3, 0), (1, 1)), own, sib, [a2, a3, b1], acc)
    ahead, back, *acc = fence((ahead, back, *acc))
    chunks = [near, ahead, get(ahead, FROM_X), back]
    kv = jnp.concatenate(chunks + [get(chunk, FROM_CORE) for chunk in chunks], 0)
    acc = project_query(blocks((2, 1), (3, 1)), own, sib, [b2, b3], acc)

    blocks_here = rows // BLK

    def where(s):
        return jnp.stack([s * blocks_here, x, z_hi, c]).astype(jnp.int32)

    out_sib = attend(sib_picks, where(seq + step), acc[1], cos_sib, sin_sib, kv, 40)
    received = get(out_sib, FROM_CORE)
    out_own = attend(picks[0], where(seq), acc[0], cos_own, sin_own, kv, 58)
    out = jnp.where(
        plain,
        jnp.concatenate([received, out_own], 1),
        jnp.concatenate([out_own, received], 1),
    )
    return out[None]


def solution(mesh):
    in_specs = (P("dp", "seq", None), P("dp", None), P("dp", None), P("dp", "seq", None))
    out_specs = P("dp", "seq", None)
    return jax.shard_map(local, mesh=mesh, in_specs=in_specs, out_specs=out_specs, check_vma=False)
```
